32 devices in a mesh: group: 2 (over y), chan: 4 (over z), stat: 2 (over x), pol: 2 (over core).
Axes of the slice: x: 2, y: 2, z: 4, core: 2. Of those that a mesh axis runs over, the one named last changes fastest.
Arguments:
- voltages: bfloat16 [4, 16, 2, 19, 2, 4096], P(('group', 'stat'), 'chan', 'pol'), parts along dimension 0, may hold values from -6 to 6
- filter_taps: float32 [12, 4096], replicated, may hold values from -1.5 to 1.5
- beam_table: float32 [2, 16], replicated, may hold values from -4 to 4
- beam_index: int32 [500, 32], replicated, may hold values from 0 to 15
- block_owner: int32 [32], replicated, may hold values from 0 to 31, each once
Outputs:
- visibilities: float32 [64, 2, 64, 64], P(('group', 'chan'), None, ('stat', 'pol')), parts along dimension 0
- beams: float32 [1000, 2, 2, 8, 4096], P(('group', 'stat'), 'pol', None, None, 'chan'), parts along dimension 0
The draws below stay inside these ranges and needn't reach their ends.
There are 2 independent parts, one for each index of `group`. The reference program is written for one: setup_inputs(seed, part) draws one part's arguments, and reference() takes and returns one part's arrays. A program takes and returns all parts, laid end to end along the dimension named above; an argument that names none is the same for every part. Nothing has to cross between parts.
Inputs may be any that keep to these rules, and one draw needn't show every extreme that they name: `block_owner`: each of the 32 channel groups appears at exactly one position.
All inputs are finite; a program needn't handle non-finite values.
Results may differ from the reference program's by a relative error of at most 0.0095.
Values may be sent and summed in bfloat16 or wider, within the bound.
A program may use at most 64 MiB of HBM per device.

```python
import math
import jax
import jax.numpy as jnp
from jax import lax

NFFT = 4096
TAPS = 12
AVG = 128
TABLE = 16
BEAMS = 500
FR = 8
BLOCKS = 19
SEC = 16
SECTIONS = 2
STATIONS = 32
INPUTS = 64
NAVG = 32


def plant(drawn, stream_key, low, largest):
    place = [jax.random.randint(jax.random.fold_in(stream_key, axis), (), 0, length) for axis, length in enumerate(drawn.shape)]
    longest = drawn.shape.index(max(drawn.shape))
    next_to = place[:longest] + [(place[longest] + 1) % drawn.shape[longest]] + place[longest + 1:]
    return drawn.at[tuple(place)].set(low).at[tuple(next_to)].set(largest)


def shard_levels(stream_key, dims, cuts, smallest, largest):
    def one(dim, parts):
        heights = jax.random.uniform(jax.random.fold_in(jax.random.fold_in(stream_key, 6), dim), (parts,), jnp.float32, smallest / len(cuts), largest / len(cuts))
        return jnp.repeat(jnp.exp(heights), dims[dim] // parts).reshape((-1,) + (1,) * (len(dims) - dim - 1))

    gain = one(*cuts[0])
    for cut in cuts[1:]:
        gain = gain * one(*cut)
    return gain


def scatter_about(key, dims, spread, bound, shards=(), held_as=jnp.bfloat16):
    entries = spread * jax.random.normal(key, dims, jnp.float32)
    if shards:
        entries = entries * shard_levels(key, dims, shards, -0.22, 0.18)
    return jnp.clip(entries, -bound, bound).astype(held_as)


def setup_inputs(seed: int = 0, part: int = 0) -> dict:
    streams_of = jax.random.split(jax.random.key(seed), 6)
    part_keys = jax.random.split(jax.random.fold_in(streams_of[5], part), 6)
    voltages = scatter_about(part_keys[0], (SECTIONS, SEC, 2, BLOCKS, 2, NFFT), 1.0, 6.0, ((0, 2), (1, 4), (2, 2)))
    filter_taps = scatter_about(streams_of[1], (TAPS, NFFT), 0.3, 1.5, (), jnp.float32)
    beam_table = scatter_about(streams_of[2], (2, TABLE), 1.0, 4.0, (), jnp.float32)
    beam_index = plant(jax.random.randint(streams_of[3], (BEAMS, STATIONS), 0, TABLE), jax.random.fold_in(streams_of[3], 1), 0, TABLE - 1).astype(jnp.int32)
    block_owner = jax.random.permutation(streams_of[4], NAVG).astype(jnp.int32)
    return {"voltages": voltages, "filter_taps": filter_taps, "beam_table": beam_table, "beam_index": beam_index, "block_owner": block_owner}


def reference(voltages, filter_taps, beam_table, beam_index, block_owner):

    def channelise(section):
        samples = section.astype(jnp.float32)
        filtered = jnp.zeros((SEC, 2, FR, 2, NFFT), jnp.float32)
        for tap_index in range(TAPS):
            filtered = filtered + filter_taps[tap_index] * samples[:, :, tap_index:tap_index + FR]
        spectrum = jnp.fft.fft(filtered[:, :, :, 0] + 1j * filtered[:, :, :, 1], axis=-1, norm='ortho')
        stacked = jnp.stack([jnp.real(spectrum), jnp.imag(spectrum)], axis=2)
        return stacked.astype(jnp.bfloat16)
    spectra = lax.map(channelise, voltages)
    blocked = spectra.reshape(SECTIONS, SEC, 2, 2, FR, NAVG, AVG)
    ordered = jnp.take(blocked, block_owner, axis=5).reshape(SECTIONS, SEC, 2, 2, FR, NFFT)
    inputs = jnp.transpose(ordered, (0, 2, 1, 3, 4, 5)).reshape(INPUTS, 2, FR, NFFT // AVG, AVG)
    channel_groups = jnp.moveaxis(inputs, 3, 0)

    def average(channel_group):
        own_rows = channel_group.reshape(INPUTS, 2 * FR * AVG)
        rotated = jnp.concatenate([-channel_group[:, 1:2], channel_group[:, 0:1]], axis=1).reshape(INPUTS, 2 * FR * AVG)
        real_part = jnp.dot(own_rows, own_rows.T, preferred_element_type=jnp.float32)
        imag_part = jnp.dot(own_rows, rotated.T, preferred_element_type=jnp.float32)
        return jnp.stack([real_part, imag_part], axis=0) * (1.0 / (FR * AVG))
    visibilities = lax.map(average, channel_groups)
    weights = (beam_table[:, beam_index] * (1.0 / math.sqrt(STATIONS))).astype(jnp.bfloat16)
    stations = ordered.reshape(STATIONS, 2, 2, FR * NFFT)

    def form_beams(polarity):
        real_in = stations[:, polarity, 0]
        imag_in = stations[:, polarity, 1]
        real_out = jnp.dot(weights[0], real_in, preferred_element_type=jnp.float32) - jnp.dot(weights[1], imag_in, preferred_element_type=jnp.float32)
        imag_out = jnp.dot(weights[1], real_in, preferred_element_type=jnp.float32) + jnp.dot(weights[0], imag_in, preferred_element_type=jnp.float32)
        return jnp.stack([real_out, imag_out], axis=1)
    beams = jnp.stack([form_beams(0), form_beams(1)], axis=1).reshape(BEAMS, 2, 2, FR, NFFT)
    return (visibilities, beams)
```

```python
import functools
import math

import jax
import jax.numpy as jnp
from jax import lax
from jax.experimental import pallas as pl
from jax.experimental.pallas import tpu as pltpu
from jax.sharding import PartitionSpec as P

ROOT = 64
AVG = 128
MESH = pl.DeviceIdType.MESH
VMEM_BYTES = 56 * 2**20


def fourier_segment(length):
    counter = jnp.arange(length, dtype=jnp.int32)
    phase = (counter[:, None] * counter[None, :] % length).astype(jnp.float32) * (
        2.0 * math.pi / length
    )
    cosine = jnp.cos(phase)
    sine = jnp.sin(phase)
    upper_half = jnp.stack([cosine, -sine], axis=1)
    lower_half = jnp.stack([sine, cosine], axis=1)
    return jnp.stack([upper_half, lower_half], axis=0)


def channelise(voltages, filter_taps):
    samples = voltages[0, :, 0].astype(jnp.float32)
    taps_count = filter_taps.shape[0]
    frames = samples.shape[1] - taps_count + 1
    filtered = filter_taps[0] * samples[:, 0:frames]
    for tap_index in range(1, taps_count):
        filtered = filtered + filter_taps[tap_index] * samples[:, tap_index : tap_index + frames]
    stations = samples.shape[0]
    shaped = filtered.reshape(stations, frames, 2, ROOT, ROOT)
    matrix = fourier_segment(ROOT)
    segment_one = jnp.einsum("sfcxy,cxdk->sfdky", shaped, matrix, precision=lax.Precision.HIGHEST)
    counter = jnp.arange(ROOT, dtype=jnp.int32)
    twiddle = (counter[:, None] * counter[None, :]).astype(jnp.float32) * (
        2.0 * math.pi / (ROOT * ROOT)
    )
    twiddle_cos = jnp.cos(twiddle)
    twiddle_sin = jnp.sin(twiddle)
    turned_real = segment_one[:, :, 0] * twiddle_cos + segment_one[:, :, 1] * twiddle_sin
    turned_imag = segment_one[:, :, 1] * twiddle_cos - segment_one[:, :, 0] * twiddle_sin
    turned = jnp.stack([turned_real, turned_imag], axis=2)
    segment_two = jnp.einsum("sfcky,cydz->sdfzk", turned, matrix, precision=lax.Precision.HIGHEST)
    return (segment_two.reshape(stations, 2, frames, ROOT * ROOT) * (1.0 / ROOT)).astype(
        jnp.bfloat16
    )


def exchange_kernel(owners, sections, y_ref, g_ref, zs, zr, xs, xr, cs, cr, own_sem):
    z = lax.axis_index("chan")
    st = lax.axis_index("stat")
    pol = lax.axis_index("pol")

    barrier = pltpu.get_barrier_semaphore()
    for o in range(1, owners):
        pl.semaphore_signal(barrier, inc=1, device_id={"chan": lax.rem(z + o, owners)}, device_id_type=MESH)
    for o in range(1, sections):
        pl.semaphore_signal(barrier, inc=1, device_id={"stat": lax.rem(st + o, sections)}, device_id_type=MESH)
    pl.semaphore_signal(barrier, inc=1, device_id={"pol": 1 - pol}, device_id_type=MESH)
    pl.semaphore_wait(barrier, owners + sections - 1)

    def to_owner(o):
        target = lax.rem(z + o, owners)
        return pltpu.make_async_remote_copy(
            src_ref=y_ref.at[target], dst_ref=g_ref.at[0, st, z],
            send_sem=zs.at[o], recv_sem=zr.at[z],
            device_id={"chan": target}, device_id_type=MESH)

    def from_owner(o):
        source = lax.rem(z - o + owners, owners)
        return pltpu.make_async_remote_copy(
            src_ref=y_ref.at[source], dst_ref=g_ref.at[0, st, source],
            send_sem=zs.at[o], recv_sem=zr.at[source],
            device_id={"chan": source}, device_id_type=MESH)

    def to_section(o, block):
        target = lax.rem(st + o, sections)
        return pltpu.make_async_remote_copy(
            src_ref=g_ref.at[0, st, block], dst_ref=g_ref.at[0, st, block],
            send_sem=xs.at[o, block], recv_sem=xr.at[st, block],
            device_id={"stat": target}, device_id_type=MESH)

    def from_section(o, block):
        source = lax.rem(st - o + sections, sections)
        return pltpu.make_async_remote_copy(
            src_ref=g_ref.at[0, source, block], dst_ref=g_ref.at[0, source, block],
            send_sem=xs.at[o, block], recv_sem=xr.at[source, block],
            device_id={"stat": source}, device_id_type=MESH)

    def to_core(o, block):
        source = lax.rem(st - o + sections, sections)
        return pltpu.make_async_remote_copy(
            src_ref=g_ref.at[0, source, block], dst_ref=g_ref.at[1, source, block],
            send_sem=cs.at[source, block], recv_sem=cr.at[source, block],
            device_id={"pol": 1 - pol}, device_id_type=MESH)

    own = pltpu.make_async_copy(y_ref.at[z], g_ref.at[0, st, z], own_sem)
    own.start()
    for o in range(1, owners):
        to_owner(o).start()
    for o in range(owners):
        block = lax.rem(z - o + owners, owners)
        if o == 0:
            own.wait()
        else:
            from_owner(o).wait_recv()
        for q in range(1, sections):
            to_section(q, block).start()
        to_core(0, block).start()
        if o:
            before = lax.rem(z - o + 1 + owners, owners)
            for q in range(1, sections):
                from_section(q, before).wait_recv()
                to_core(q, before).start()
    last = lax.rem(z + 1, owners)
    for q in range(1, sections):
        from_section(q, last).wait_recv()
        to_core(q, last).start()
    for o in range(owners):
        for q in range(sections):
            to_core(q, lax.rem(z - o + owners, owners)).wait()
    for o in range(1, owners):
        to_owner(o).wait_send()
    for o in range(owners):
        for q in range(1, sections):
            to_section(q, lax.rem(z - o + owners, owners)).wait_send()


def exchange(blocks, owners, sections):
    return pl.pallas_call(
        functools.partial(exchange_kernel, owners, sections),
        out_shape=jax.ShapeDtypeStruct((2, sections) + blocks.shape, blocks.dtype),
        in_specs=[pl.BlockSpec(memory_space=pl.ANY)],
        out_specs=pl.BlockSpec(memory_space=pl.ANY),
        scratch_shapes=[
            pltpu.SemaphoreType.DMA((owners,)),
            pltpu.SemaphoreType.DMA((owners,)),
            pltpu.SemaphoreType.DMA((sections, owners)),
            pltpu.SemaphoreType.DMA((sections, owners)),
            pltpu.SemaphoreType.DMA((sections, owners)),
            pltpu.SemaphoreType.DMA((sections, owners)),
            pltpu.SemaphoreType.DMA,
        ],
        compiler_params=pltpu.CompilerParams(collective_id=0, has_side_effects=True),
        name="exchange",
    )(blocks)


def iota(shape, dim):
    return lax.broadcasted_iota(jnp.int32, shape, dim)


def product_kernel(frames, stations, mean_factor, place_ref, w_ref, col_ref, g_ref, vis_ref, out_ref, x_ref):
    _, sections, owners, groups, rows, _ = g_ref.shape
    step = pl.program_id(0)
    depth = sections * owners * rows
    pair = 4 * stations

    @pl.when(step == 0)
    def _():
        for a in range(groups):
            x_ref[:, a * AVG : (a + 1) * AVG] = g_ref[0, :, :, a].reshape(depth, AVG)

    nb = w_ref.shape[1]
    wide = jnp.dot(w_ref[0], col_ref[...], preferred_element_type=jnp.float32)
    column = iota((frames, depth), 1)
    same = lax.rem(lax.div(column, 2 * stations), frames) == iota((frames, depth), 0)
    spread = jnp.where(same[None], wide[:, None, :], 0.0).reshape(nb * frames, depth)
    out_ref[...] = jnp.dot(spread.astype(jnp.bfloat16), x_ref[...], preferred_element_type=jnp.float32)

    @pl.when(step == pl.num_programs(0) - 1)
    def _():
        st = place_ref[0]
        pol = place_ref[1]
        m = owners * pair
        n = sections * owners * pair
        own_count = owners * stations
        row = iota((m, n), 0)
        col = iota((m, n), 1)
        par = 2 * stations
        same_par = lax.rem(lax.div(row, par), 2) == lax.rem(lax.div(col, par), 2)
        rc = lax.rem(row, 2)
        cc = lax.rem(col, 2)
        re_mask = jnp.where(same_par & (rc == cc), mean_factor, 0.0)
        im_mask = jnp.where(same_par & (rc != cc), jnp.where(rc == 1, mean_factor, -mean_factor), 0.0)

        def station(i):
            return lax.div(i, pair) * stations + lax.rem(lax.div(i, 2), stations)

        left = (station(iota((own_count, m), 1)) == iota((own_count, m), 0)).astype(jnp.float32)
        inputs = sections * 2 * own_count
        for p in range(2):
            q = jnp.where(pol == 0, p, 1 - p)
            i = iota((n, inputs), 0)
            sec = lax.div(i, m)
            where = sec * (2 * own_count) + q * own_count + station(lax.rem(i, m))
            right = (where == iota((n, inputs), 1)).astype(jnp.float32)
            halves = []
            for a in range(groups):
                raw = jnp.zeros((m, n), jnp.float32)
                for f in range(rows // pair):
                    mine = g_ref[0, st, :, a, f * pair : (f + 1) * pair].reshape(m, AVG)
                    theirs = g_ref[p, :, :, a, f * pair : (f + 1) * pair].reshape(n, AVG)
                    raw = raw + lax.dot_general(
                        mine, theirs, (((1,), (1,)), ((), ())), preferred_element_type=jnp.float32
                    )
                for mask in (re_mask, im_mask):
                    halves.append(
                        jnp.dot(left, raw * mask, precision=lax.Precision.HIGHEST, preferred_element_type=jnp.float32)
                    )
            total = jnp.dot(
                jnp.concatenate(halves, axis=0), right,
                precision=lax.Precision.HIGHEST, preferred_element_type=jnp.float32,
            ).reshape(groups, 2, own_count, inputs)
            if p == 0:
                vis_ref[...] = total
            else:
                vis_ref[...] += total


def products(gathered, weights, frames, stations, mean_factor):
    _, sections, owners, groups, rows, _ = gathered.shape
    depth = sections * owners * rows
    width = groups * AVG
    count = weights.shape[0]
    nb = 50
    while count % nb or nb * frames * depth > 400 * 1024:
        nb -= 1
    blocks = count // nb
    row = jnp.arange(weights.shape[1], dtype=jnp.int32)[:, None]
    col = jnp.arange(depth, dtype=jnp.int32)[None, :]
    names = (col % 2) * (sections * owners * stations) + (col // rows) * stations + (col // 2) % stations
    spread = (row == names).astype(jnp.bfloat16)
    place = jnp.stack([lax.axis_index("stat"), lax.axis_index("pol")]).astype(jnp.int32)
    own_count = owners * stations
    vis, beams = pl.pallas_call(
        functools.partial(product_kernel, frames, stations, mean_factor),
        grid=(blocks,),
        in_specs=[
            pl.BlockSpec(memory_space=pltpu.SMEM),
            pl.BlockSpec((1, nb, weights.shape[1]), lambda i: (i, 0, 0)),
            pl.BlockSpec(memory_space=pltpu.VMEM),
            pl.BlockSpec(memory_space=pltpu.VMEM),
        ],
        out_specs=[
            pl.BlockSpec(memory_space=pltpu.VMEM),
            pl.BlockSpec((nb * frames, width), lambda i: (i, 0)),
        ],
        out_shape=[
            jax.ShapeDtypeStruct((groups, 2, own_count, 2 * sections * own_count), jnp.float32),
            jax.ShapeDtypeStruct((count * frames, width), jnp.float32),
        ],
        scratch_shapes=[pltpu.VMEM((depth, width), jnp.bfloat16)],
        compiler_params=pltpu.CompilerParams(vmem_limit_bytes=VMEM_BYTES),
        name="products",
    )(place, weights.reshape(blocks, nb, weights.shape[1]), spread, gathered)
    return vis, beams


def beam_weights(indices, beam_table, factor):
    levels = jnp.arange(beam_table.shape[1], dtype=jnp.int32)
    selected = indices[..., None] == levels
    w_real = jnp.sum(jnp.where(selected, beam_table[0], 0.0), axis=-1) * factor
    w_imag = jnp.sum(jnp.where(selected, beam_table[1], 0.0), axis=-1) * factor
    upper_half = jnp.concatenate([w_real, -w_imag], axis=1)
    lower_half = jnp.concatenate([w_imag, w_real], axis=1)
    return jnp.stack([upper_half, lower_half], axis=1).astype(jnp.bfloat16)


def on_device(voltages, filter_taps, beam_table, beam_index, block_owner):
    owners = lax.axis_size("chan")
    sections = lax.axis_size("stat")
    spectra = channelise(voltages, filter_taps)
    stations, _, frames, nfft = spectra.shape
    group_count = block_owner.shape[0]
    grouped = spectra.reshape(stations, 2, frames, group_count, AVG)
    regrouped = jnp.take(grouped, block_owner, axis=3)
    groups = group_count // owners
    blocks = jnp.transpose(regrouped, (3, 2, 0, 1, 4)).reshape(
        owners, groups, frames * stations * 2, AVG
    )
    gathered = exchange(blocks, owners, sections)
    section = lax.axis_index("stat")
    beam_count, station_count = beam_index.shape
    owned = beam_count // sections
    own_index = lax.dynamic_slice_in_dim(beam_index, section * owned, owned, 0)
    weights = beam_weights(own_index, beam_table, 1.0 / math.sqrt(station_count))
    vis, beams = products(
        gathered, weights.reshape(owned * 2, 2 * station_count), frames, stations, 1.0 / (frames * AVG)
    )
    return vis, beams.reshape(owned, 1, 2, frames, groups * AVG)


def solution(mesh):
    return jax.shard_map(
        on_device,
        mesh=mesh,
        in_specs=(P(("group", "stat"), "chan", "pol", None, None, None), P(), P(), P(), P()),
        out_specs=(
            P(("group", "chan"), None, ("stat", "pol"), None),
            P(("group", "stat"), "pol", None, None, "chan"),
        ),
        check_vma=False,
    )
```

```python
import functools
import math

import jax
import jax.numpy as jnp
from jax import lax
from jax.experimental import pallas as pl
from jax.experimental.pallas import tpu as pltpu
from jax.sharding import PartitionSpec as P

ROOT = 64
AVG = 128
MESH = pl.DeviceIdType.MESH
VMEM_BYTES = 56 * 2**20


def fourier_segment(length):
    counter = jnp.arange(length, dtype=jnp.int32)
    phase = (counter[:, None] * counter[None, :] % length).astype(jnp.float32) * (
        2.0 * math.pi / length
    )
    cosine = jnp.cos(phase)
    sine = jnp.sin(phase)
    upper_half = jnp.stack([cosine, -sine], axis=1)
    lower_half = jnp.stack([sine, cosine], axis=1)
    return jnp.stack([upper_half, lower_half], axis=0)


def channelise(voltages, filter_taps):
    samples = voltages[0, :, 0].astype(jnp.float32)
    taps_count = filter_taps.shape[0]
    frames = samples.shape[1] - taps_count + 1
    filtered = filter_taps[0] * samples[:, 0:frames]
    for tap_index in range(1, taps_count):
        filtered = filtered + filter_taps[tap_index] * samples[:, tap_index : tap_index + frames]
    stations = samples.shape[0]
    shaped = filtered.reshape(stations, frames, 2, ROOT, ROOT)
    matrix = fourier_segment(ROOT)
    segment_one = jnp.einsum("sfcxy,cxdk->sfdky", shaped, matrix, precision=lax.Precision.DEFAULT)
    counter = jnp.arange(ROOT, dtype=jnp.int32)
    twiddle = (counter[:, None] * counter[None, :]).astype(jnp.float32) * (
        2.0 * math.pi / (ROOT * ROOT)
    )
    twiddle_cos = jnp.cos(twiddle)
    twiddle_sin = jnp.sin(twiddle)
    turned_real = segment_one[:, :, 0] * twiddle_cos + segment_one[:, :, 1] * twiddle_sin
    turned_imag = segment_one[:, :, 1] * twiddle_cos - segment_one[:, :, 0] * twiddle_sin
    turned = jnp.stack([turned_real, turned_imag], axis=2)
    segment_two = jnp.einsum("sfcky,cydz->sdfzk", turned, matrix, precision=lax.Precision.DEFAULT)
    return (segment_two.reshape(stations, 2, frames, ROOT * ROOT) * (1.0 / ROOT)).astype(
        jnp.bfloat16
    )


def exchange_kernel(owners, sections, y_ref, g_ref, zs, zr, xs, xr, cs, cr, own_sem):
    z = lax.axis_index("chan")
    st = lax.axis_index("stat")
    pol = lax.axis_index("pol")

    barrier = pltpu.get_barrier_semaphore()
    for o in range(1, owners):
        pl.semaphore_signal(barrier, inc=1, device_id={"chan": lax.rem(z + o, owners)}, device_id_type=MESH)
    for o in range(1, sections):
        pl.semaphore_signal(barrier, inc=1, device_id={"stat": lax.rem(st + o, sections)}, device_id_type=MESH)
    pl.semaphore_signal(barrier, inc=1, device_id={"pol": 1 - pol}, device_id_type=MESH)
    pl.semaphore_wait(barrier, owners + sections - 1)

    def to_owner(o):
        target = lax.rem(z + o, owners)
        return pltpu.make_async_remote_copy(
            src_ref=y_ref.at[target], dst_ref=g_ref.at[0, st, z],
            send_sem=zs.at[o], recv_sem=zr.at[z],
            device_id={"chan": target}, device_id_type=MESH)

    def from_owner(o):
        source = lax.rem(z - o + owners, owners)
        return pltpu.make_async_remote_copy(
            src_ref=y_ref.at[source], dst_ref=g_ref.at[0, st, source],
            send_sem=zs.at[o], recv_sem=zr.at[source],
            device_id={"chan": source}, device_id_type=MESH)

    def to_section(o, block):
        target = lax.rem(st + o, sections)
        return pltpu.make_async_remote_copy(
            src_ref=g_ref.at[0, st, block], dst_ref=g_ref.at[0, st, block],
            send_sem=xs.at[o, block], recv_sem=xr.at[st, block],
            device_id={"stat": target}, device_id_type=MESH)

    def from_section(o, block):
        source = lax.rem(st - o + sections, sections)
        return pltpu.make_async_remote_copy(
            src_ref=g_ref.at[0, source, block], dst_ref=g_ref.at[0, source, block],
            send_sem=xs.at[o, block], recv_sem=xr.at[source, block],
            device_id={"stat": source}, device_id_type=MESH)

    def to_core(o, block):
        source = lax.rem(st - o + sections, sections)
        return pltpu.make_async_remote_copy(
            src_ref=g_ref.at[0, source, block], dst_ref=g_ref.at[1, source, block],
            send_sem=cs.at[source, block], recv_sem=cr.at[source, block],
            device_id={"pol": 1 - pol}, device_id_type=MESH)

    own = pltpu.make_async_copy(y_ref.at[z], g_ref.at[0, st, z], own_sem)
    own.start()
    for o in range(1, owners):
        to_owner(o).start()
    for o in range(owners):
        block = lax.rem(z - o + owners, owners)
        if o == 0:
            own.wait()
        else:
            from_owner(o).wait_recv()
        for q in range(1, sections):
            to_section(q, block).start()
        to_core(0, block).start()
        if o:
            before = lax.rem(z - o + 1 + owners, owners)
            for q in range(1, sections):
                from_section(q, before).wait_recv()
                to_core(q, before).start()
    last = lax.rem(z + 1, owners)
    for q in range(1, sections):
        from_section(q, last).wait_recv()
        to_core(q, last).start()
    for o in range(owners):
        for q in range(sections):
            to_core(q, lax.rem(z - o + owners, owners)).wait()
    for o in range(1, owners):
        to_owner(o).wait_send()
    for o in range(owners):
        for q in range(1, sections):
            to_section(q, lax.rem(z - o + owners, owners)).wait_send()


def exchange(blocks, owners, sections):
    return pl.pallas_call(
        functools.partial(exchange_kernel, owners, sections),
        out_shape=jax.ShapeDtypeStruct((2, sections) + blocks.shape, blocks.dtype),
        in_specs=[pl.BlockSpec(memory_space=pl.ANY)],
        out_specs=pl.BlockSpec(memory_space=pl.ANY),
        scratch_shapes=[
            pltpu.SemaphoreType.DMA((owners,)),
            pltpu.SemaphoreType.DMA((owners,)),
            pltpu.SemaphoreType.DMA((sections, owners)),
            pltpu.SemaphoreType.DMA((sections, owners)),
            pltpu.SemaphoreType.DMA((sections, owners)),
            pltpu.SemaphoreType.DMA((sections, owners)),
            pltpu.SemaphoreType.DMA,
        ],
        compiler_params=pltpu.CompilerParams(collective_id=0, has_side_effects=True),
        name="exchange",
    )(blocks)


def iota(shape, dim):
    return lax.broadcasted_iota(jnp.int32, shape, dim)


def product_kernel(frames, stations, mean_factor, place_ref, w_ref, col_ref, g_ref, vis_ref, out_ref, x_ref):
    _, sections, owners, groups, rows, _ = g_ref.shape
    step = pl.program_id(0)
    depth = sections * owners * rows
    pair = 4 * stations

    @pl.when(step == 0)
    def _():
        for a in range(groups):
            x_ref[:, a * AVG : (a + 1) * AVG] = g_ref[0, :, :, a].reshape(depth, AVG)

    nb = w_ref.shape[1]
    wide = jnp.dot(w_ref[0], col_ref[...], preferred_element_type=jnp.float32)
    column = iota((frames, depth), 1)
    same = lax.rem(lax.div(column, 2 * stations), frames) == iota((frames, depth), 0)
    spread = jnp.where(same[None], wide[:, None, :], 0.0).reshape(nb * frames, depth)
    out_ref[...] = jnp.dot(spread.astype(jnp.bfloat16), x_ref[...], preferred_element_type=jnp.float32)

    @pl.when(step == pl.num_programs(0) - 1)
    def _():
        st = place_ref[0]
        pol = place_ref[1]
        m = owners * pair
        n = sections * owners * pair
        own_count = owners * stations
        row = iota((m, n), 0)
        col = iota((m, n), 1)
        par = 2 * stations
        same_par = lax.rem(lax.div(row, par), 2) == lax.rem(lax.div(col, par), 2)
        rc = lax.rem(row, 2)
        cc = lax.rem(col, 2)
        re_mask = jnp.where(same_par & (rc == cc), mean_factor, 0.0)
        im_mask = jnp.where(same_par & (rc != cc), jnp.where(rc == 1, mean_factor, -mean_factor), 0.0)

        def station(i):
            return lax.div(i, pair) * stations + lax.rem(lax.div(i, 2), stations)

        lr = iota((2 * groups * own_count, 2 * groups * m), 0)
        lc = iota((2 * groups * own_count, 2 * groups * m), 1)
        left = (lax.div(lc, m) * own_count + station(lax.rem(lc, m)) == lr).astype(jnp.float32)
        inputs = sections * 2 * own_count
        for p in range(2):
            q = jnp.where(pol == 0, p, 1 - p)
            i = iota((n, inputs), 0)
            sec = lax.div(i, m)
            where = sec * (2 * own_count) + q * own_count + station(lax.rem(i, m))
            right = (where == iota((n, inputs), 1)).astype(jnp.float32)
            halves = []
            for a in range(groups):
                raw = jnp.zeros((m, n), jnp.float32)
                for f in range(rows // pair):
                    mine = g_ref[0, st, :, a, f * pair : (f + 1) * pair].reshape(m, AVG)
                    theirs = g_ref[p, :, :, a, f * pair : (f + 1) * pair].reshape(n, AVG)
                    raw = raw + lax.dot_general(
                        mine, theirs, (((1,), (1,)), ((), ())), preferred_element_type=jnp.float32
                    )
                halves += [raw * re_mask, raw * im_mask]
            columns = jnp.dot(
                jnp.concatenate(halves, axis=0), right,
                precision=lax.Precision.HIGHEST, preferred_element_type=jnp.float32,
            )
            total = jnp.dot(
                left, columns, precision=lax.Precision.HIGHEST, preferred_element_type=jnp.float32
            ).reshape(groups, 2, own_count, inputs)
            if p == 0:
                vis_ref[...] = total
            else:
                vis_ref[...] += total


def products(gathered, weights, frames, stations, mean_factor):
    _, sections, owners, groups, rows, _ = gathered.shape
    depth = sections * owners * rows
    width = groups * AVG
    count = weights.shape[0]
    nb = 50
    while count % nb or nb * frames * depth > 400 * 1024:
        nb -= 1
    blocks = count // nb
    row = jnp.arange(weights.shape[1], dtype=jnp.int32)[:, None]
    col = jnp.arange(depth, dtype=jnp.int32)[None, :]
    names = (col % 2) * (sections * owners * stations) + (col // rows) * stations + (col // 2) % stations
    spread = (row == names).astype(jnp.bfloat16)
    place = jnp.stack([lax.axis_index("stat"), lax.axis_index("pol")]).astype(jnp.int32)
    own_count = owners * stations
    vis, beams = pl.pallas_call(
        functools.partial(product_kernel, frames, stations, mean_factor),
        grid=(blocks,),
        in_specs=[
            pl.BlockSpec(memory_space=pltpu.SMEM),
            pl.BlockSpec((1, nb, weights.shape[1]), lambda i: (i, 0, 0)),
            pl.BlockSpec(memory_space=pltpu.VMEM),
            pl.BlockSpec(memory_space=pltpu.VMEM),
        ],
        out_specs=[
            pl.BlockSpec(memory_space=pltpu.VMEM),
            pl.BlockSpec((nb * frames, width), lambda i: (i, 0)),
        ],
        out_shape=[
            jax.ShapeDtypeStruct((groups, 2, own_count, 2 * sections * own_count), jnp.float32),
            jax.ShapeDtypeStruct((count * frames, width), jnp.float32),
        ],
        scratch_shapes=[pltpu.VMEM((depth, width), jnp.bfloat16)],
        compiler_params=pltpu.CompilerParams(vmem_limit_bytes=VMEM_BYTES),
        name="products",
    )(place, weights.reshape(blocks, nb, weights.shape[1]), spread, gathered)
    return vis, beams


def beam_weights(indices, beam_table, factor):
    levels = jnp.arange(beam_table.shape[1], dtype=jnp.int32)
    selected = indices[..., None] == levels
    w_real = jnp.sum(jnp.where(selected, beam_table[0], 0.0), axis=-1) * factor
    w_imag = jnp.sum(jnp.where(selected, beam_table[1], 0.0), axis=-1) * factor
    upper_half = jnp.concatenate([w_real, -w_imag], axis=1)
    lower_half = jnp.concatenate([w_imag, w_real], axis=1)
    return jnp.stack([upper_half, lower_half], axis=1).astype(jnp.bfloat16)


def on_device(voltages, filter_taps, beam_table, beam_index, block_owner):
    owners = lax.axis_size("chan")
    sections = lax.axis_size("stat")
    spectra = channelise(voltages, filter_taps)
    stations, _, frames, nfft = spectra.shape
    group_count = block_owner.shape[0]
    grouped = spectra.reshape(stations, 2, frames, group_count, AVG)
    regrouped = jnp.take(grouped, block_owner, axis=3)
    groups = group_count // owners
    blocks = jnp.transpose(regrouped, (3, 2, 0, 1, 4)).reshape(
        owners, groups, frames * stations * 2, AVG
    )
    gathered = exchange(blocks, owners, sections)
    section = lax.axis_index("stat")
    beam_count, station_count = beam_index.shape
    owned = beam_count // sections
    own_index = lax.dynamic_slice_in_dim(beam_index, section * owned, owned, 0)
    weights = beam_weights(own_index, beam_table, 1.0 / math.sqrt(station_count))
    vis, beams = products(
        gathered, weights.reshape(owned * 2, 2 * station_count), frames, stations, 1.0 / (frames * AVG)
    )
    return vis, beams.reshape(owned, 1, 2, frames, groups * AVG)


def solution(mesh):
    return jax.shard_map(
        on_device,
        mesh=mesh,
        in_specs=(P(("group", "stat"), "chan", "pol", None, None, None), P(), P(), P(), P()),
        out_specs=(
            P(("group", "chan"), None, ("stat", "pol"), None),
            P(("group", "stat"), "pol", None, None, "chan"),
        ),
        check_vma=False,
    )
```

```python
import functools
import math

import jax
import jax.numpy as jnp
from jax import lax
from jax.experimental import pallas as pl
from jax.experimental.pallas import tpu as pltpu
from jax.sharding import PartitionSpec as P

ROOT = 64
AVG = 128
MESH = pl.DeviceIdType.MESH
VMEM_BYTES = 56 * 2**20


def fourier_segment(length):
    counter = jnp.arange(length, dtype=jnp.int32)
    phase = (counter[:, None] * counter[None, :] % length).astype(jnp.float32) * (
        2.0 * math.pi / length
    )
    cosine = jnp.cos(phase)
    sine = jnp.sin(phase)
    upper_half = jnp.stack([cosine, -sine], axis=1)
    lower_half = jnp.stack([sine, cosine], axis=1)
    return jnp.stack([upper_half, lower_half], axis=0)


def channelise(voltages, filter_taps):
    samples = voltages[0, :, 0].astype(jnp.float32)
    taps_count = filter_taps.shape[0]
    frames = samples.shape[1] - taps_count + 1
    filtered = filter_taps[0] * samples[:, 0:frames]
    for tap_index in range(1, taps_count):
        filtered = filtered + filter_taps[tap_index] * samples[:, tap_index : tap_index + frames]
    stations = samples.shape[0]
    shaped = filtered.reshape(stations, frames, 2, ROOT, ROOT)
    matrix = fourier_segment(ROOT)
    segment_one = jnp.einsum("sfcxy,cxdk->sfdky", shaped, matrix, precision=lax.Precision.DEFAULT)
    counter = jnp.arange(ROOT, dtype=jnp.int32)
    twiddle = (counter[:, None] * counter[None, :]).astype(jnp.float32) * (
        2.0 * math.pi / (ROOT * ROOT)
    )
    twiddle_cos = jnp.cos(twiddle)
    twiddle_sin = jnp.sin(twiddle)
    turned_real = segment_one[:, :, 0] * twiddle_cos + segment_one[:, :, 1] * twiddle_sin
    turned_imag = segment_one[:, :, 1] * twiddle_cos - segment_one[:, :, 0] * twiddle_sin
    turned = jnp.stack([turned_real, turned_imag], axis=2)
    segment_two = jnp.einsum("sfcky,cydz->sdfzk", turned, matrix, precision=lax.Precision.DEFAULT)
    return (segment_two.reshape(stations, 2, frames, ROOT * ROOT) * (1.0 / ROOT)).astype(
        jnp.bfloat16
    )


def exchange_kernel(owners, sections, y_ref, g_ref, zs, zr, xs, xr, cs, cr, own_sem):
    z = lax.axis_index("chan")
    st = lax.axis_index("stat")
    pol = lax.axis_index("pol")

    barrier = pltpu.get_barrier_semaphore()
    for o in range(1, owners):
        pl.semaphore_signal(barrier, inc=1, device_id={"chan": lax.rem(z + o, owners)}, device_id_type=MESH)
    for o in range(1, sections):
        pl.semaphore_signal(barrier, inc=1, device_id={"stat": lax.rem(st + o, sections)}, device_id_type=MESH)
    pl.semaphore_signal(barrier, inc=1, device_id={"pol": 1 - pol}, device_id_type=MESH)
    pl.semaphore_wait(barrier, owners + sections - 1)

    def to_owner(o):
        target = lax.rem(z + o, owners)
        return pltpu.make_async_remote_copy(
            src_ref=y_ref.at[target], dst_ref=g_ref.at[0, st, z],
            send_sem=zs.at[o], recv_sem=zr.at[z],
            device_id={"chan": target}, device_id_type=MESH)

    def from_owner(o):
        source = lax.rem(z - o + owners, owners)
        return pltpu.make_async_remote_copy(
            src_ref=y_ref.at[source], dst_ref=g_ref.at[0, st, source],
            send_sem=zs.at[o], recv_sem=zr.at[source],
            device_id={"chan": source}, device_id_type=MESH)

    def to_section(o, block):
        target = lax.rem(st + o, sections)
        return pltpu.make_async_remote_copy(
            src_ref=g_ref.at[0, st, block], dst_ref=g_ref.at[0, st, block],
            send_sem=xs.at[o, block], recv_sem=xr.at[st, block],
            device_id={"stat": target}, device_id_type=MESH)

    def from_section(o, block):
        source = lax.rem(st - o + sections, sections)
        return pltpu.make_async_remote_copy(
            src_ref=g_ref.at[0, source, block], dst_ref=g_ref.at[0, source, block],
            send_sem=xs.at[o, block], recv_sem=xr.at[source, block],
            device_id={"stat": source}, device_id_type=MESH)

    def to_core(o, block):
        source = lax.rem(st - o + sections, sections)
        return pltpu.make_async_remote_copy(
            src_ref=g_ref.at[0, source, block], dst_ref=g_ref.at[1, source, block],
            send_sem=cs.at[source, block], recv_sem=cr.at[source, block],
            device_id={"pol": 1 - pol}, device_id_type=MESH)

    own = pltpu.make_async_copy(y_ref.at[z], g_ref.at[0, st, z], own_sem)
    own.start()
    for o in range(1, owners):
        to_owner(o).start()
    for o in range(owners):
        block = lax.rem(z - o + owners, owners)
        if o == 0:
            own.wait()
        else:
            from_owner(o).wait_recv()
        for q in range(1, sections):
            to_section(q, block).start()
        to_core(0, block).start()
        if o:
            before = lax.rem(z - o + 1 + owners, owners)
            for q in range(1, sections):
                from_section(q, before).wait_recv()
                to_core(q, before).start()
    last = lax.rem(z + 1, owners)
    for q in range(1, sections):
        from_section(q, last).wait_recv()
        to_core(q, last).start()
    for o in range(owners):
        for q in range(sections):
            to_core(q, lax.rem(z - o + owners, owners)).wait()
    for o in range(1, owners):
        to_owner(o).wait_send()
    for o in range(owners):
        for q in range(1, sections):
            to_section(q, lax.rem(z - o + owners, owners)).wait_send()


def exchange(blocks, owners, sections):
    return pl.pallas_call(
        functools.partial(exchange_kernel, owners, sections),
        out_shape=jax.ShapeDtypeStruct((2, sections) + blocks.shape, blocks.dtype),
        in_specs=[pl.BlockSpec(memory_space=pl.ANY)],
        out_specs=pl.BlockSpec(memory_space=pl.ANY),
        scratch_shapes=[
            pltpu.SemaphoreType.DMA((owners,)),
            pltpu.SemaphoreType.DMA((owners,)),
            pltpu.SemaphoreType.DMA((sections, owners)),
            pltpu.SemaphoreType.DMA((sections, owners)),
            pltpu.SemaphoreType.DMA((sections, owners)),
            pltpu.SemaphoreType.DMA((sections, owners)),
            pltpu.SemaphoreType.DMA,
        ],
        compiler_params=pltpu.CompilerParams(collective_id=0, has_side_effects=True),
        name="exchange",
    )(blocks)


def iota(shape, dim):
    return lax.broadcasted_iota(jnp.int32, shape, dim)


def product_kernel(frames, stations, mean_factor, place_ref, w_ref, col_ref, g_ref, vis_ref, out_ref, x_ref):
    _, sections, owners, groups, rows, _ = g_ref.shape
    step = pl.program_id(0)
    depth = sections * owners * rows
    pair = 4 * stations

    @pl.when(step == 0)
    def _():
        for a in range(groups):
            x_ref[:, a * AVG : (a + 1) * AVG] = g_ref[0, :, :, a].reshape(depth, AVG)

    nb = w_ref.shape[1]
    wide = jnp.dot(w_ref[0], col_ref[...], preferred_element_type=jnp.float32)
    column = iota((frames, depth), 1)
    same = lax.rem(lax.div(column, 2 * stations), frames) == iota((frames, depth), 0)
    spread = jnp.where(same[None], wide[:, None, :], 0.0).reshape(nb * frames, depth)
    out_ref[...] = jnp.dot(spread.astype(jnp.bfloat16), x_ref[...], preferred_element_type=jnp.float32)

    @pl.when(step == pl.num_programs(0) - 1)
    def _():
        st = place_ref[0]
        pol = place_ref[1]
        m = owners * pair
        n = sections * owners * pair
        own_count = owners * stations
        row = iota((m, n), 0)
        col = iota((m, n), 1)
        par = 2 * stations
        same_par = lax.rem(lax.div(row, par), 2) == lax.rem(lax.div(col, par), 2)
        rc = lax.rem(row, 2)
        cc = lax.rem(col, 2)
        re_mask = jnp.where(same_par & (rc == cc), mean_factor, 0.0)
        im_mask = jnp.where(same_par & (rc != cc), jnp.where(rc == 1, mean_factor, -mean_factor), 0.0)

        def station(i):
            return lax.div(i, pair) * stations + lax.rem(lax.div(i, 2), stations)

        left = (station(iota((own_count, m), 1)) == iota((own_count, m), 0)).astype(jnp.float32)
        inputs = sections * 2 * own_count
        for p in range(2):
            q = jnp.where(pol == 0, p, 1 - p)
            i = iota((n, inputs), 0)
            sec = lax.div(i, m)
            where = sec * (2 * own_count) + q * own_count + station(lax.rem(i, m))
            right = (where == iota((n, inputs), 1)).astype(jnp.float32)
            halves = []
            for a in range(groups):
                raw = jnp.zeros((m, n), jnp.float32)
                for f in range(rows // pair):
                    mine = g_ref[0, st, :, a, f * pair : (f + 1) * pair].reshape(m, AVG)
                    theirs = g_ref[p, :, :, a, f * pair : (f + 1) * pair].reshape(n, AVG)
                    raw = raw + lax.dot_general(
                        mine, theirs, (((1,), (1,)), ((), ())), preferred_element_type=jnp.float32
                    )
                for mask in (re_mask, im_mask):
                    halves.append(
                        jnp.dot(left, raw * mask, precision=lax.Precision.HIGHEST, preferred_element_type=jnp.float32)
                    )
            total = jnp.dot(
                jnp.concatenate(halves, axis=0), right,
                precision=lax.Precision.HIGHEST, preferred_element_type=jnp.float32,
            ).reshape(groups, 2, own_count, inputs)
            if p == 0:
                vis_ref[...] = total
            else:
                vis_ref[...] += total


def products(gathered, weights, frames, stations, mean_factor):
    _, sections, owners, groups, rows, _ = gathered.shape
    depth = sections * owners * rows
    width = groups * AVG
    count = weights.shape[0]
    nb = 50
    while count % nb or nb * frames * depth > 400 * 1024:
        nb -= 1
    blocks = count // nb
    row = jnp.arange(weights.shape[1], dtype=jnp.int32)[:, None]
    col = jnp.arange(depth, dtype=jnp.int32)[None, :]
    names = (col % 2) * (sections * owners * stations) + (col // rows) * stations + (col // 2) % stations
    spread = (row == names).astype(jnp.bfloat16)
    place = jnp.stack([lax.axis_index("stat"), lax.axis_index("pol")]).astype(jnp.int32)
    own_count = owners * stations
    vis, beams = pl.pallas_call(
        functools.partial(product_kernel, frames, stations, mean_factor),
        grid=(blocks,),
        in_specs=[
            pl.BlockSpec(memory_space=pltpu.SMEM),
            pl.BlockSpec((1, nb, weights.shape[1]), lambda i: (i, 0, 0)),
            pl.BlockSpec(memory_space=pltpu.VMEM),
            pl.BlockSpec(memory_space=pltpu.VMEM),
        ],
        out_specs=[
            pl.BlockSpec(memory_space=pltpu.VMEM),
            pl.BlockSpec((nb * frames, width), lambda i: (i, 0)),
        ],
        out_shape=[
            jax.ShapeDtypeStruct((groups, 2, own_count, 2 * sections * own_count), jnp.float32),
            jax.ShapeDtypeStruct((count * frames, width), jnp.float32),
        ],
        scratch_shapes=[pltpu.VMEM((depth, width), jnp.bfloat16)],
        compiler_params=pltpu.CompilerParams(vmem_limit_bytes=VMEM_BYTES),
        name="products",
    )(place, weights.reshape(blocks, nb, weights.shape[1]), spread, gathered)
    return vis, beams


def beam_weights(indices, beam_table, factor):
    levels = jnp.arange(beam_table.shape[1], dtype=jnp.int32)
    selected = indices[..., None] == levels
    w_real = jnp.sum(jnp.where(selected, beam_table[0], 0.0), axis=-1) * factor
    w_imag = jnp.sum(jnp.where(selected, beam_table[1], 0.0), axis=-1) * factor
    upper_half = jnp.concatenate([w_real, -w_imag], axis=1)
    lower_half = jnp.concatenate([w_imag, w_real], axis=1)
    return jnp.stack([upper_half, lower_half], axis=1).astype(jnp.bfloat16)


def on_device(voltages, filter_taps, beam_table, beam_index, block_owner):
    owners = lax.axis_size("chan")
    sections = lax.axis_size("stat")
    spectra = channelise(voltages, filter_taps)
    stations, _, frames, nfft = spectra.shape
    group_count = block_owner.shape[0]
    grouped = spectra.reshape(stations, 2, frames, group_count, AVG)
    regrouped = jnp.take(grouped, block_owner, axis=3)
    groups = group_count // owners
    blocks = jnp.transpose(regrouped, (3, 2, 0, 1, 4)).reshape(
        owners, groups, frames * stations * 2, AVG
    )
    gathered = exchange(blocks, owners, sections)
    section = lax.axis_index("stat")
    beam_count, station_count = beam_index.shape
    owned = beam_count // sections
    own_index = lax.dynamic_slice_in_dim(beam_index, section * owned, owned, 0)
    weights = beam_weights(own_index, beam_table, 1.0 / math.sqrt(station_count))
    vis, beams = products(
        gathered, weights.reshape(owned * 2, 2 * station_count), frames, stations, 1.0 / (frames * AVG)
    )
    return vis, beams.reshape(owned, 1, 2, frames, groups * AVG)


def solution(mesh):
    return jax.shard_map(
        on_device,
        mesh=mesh,
        in_specs=(P(("group", "stat"), "chan", "pol", None, None, None), P(), P(), P(), P()),
        out_specs=(
            P(("group", "chan"), None, ("stat", "pol"), None),
            P(("group", "stat"), "pol", None, None, "chan"),
        ),
        check_vma=False,
    )
```

```python
import functools
import math

import jax
import jax.numpy as jnp
import numpy as np
from jax import lax
from jax.experimental import pallas as pl
from jax.experimental.pallas import tpu as pltpu
from jax.sharding import PartitionSpec as P

ROOT = 64
AVG = 128
MESH = pl.DeviceIdType.MESH
VMEM_BYTES = 56 * 2**20


def fourier_segment(length):
    counter = np.arange(length, dtype=np.int32)
    phase = (counter[:, None] * counter[None, :] % length) * (
        2.0 * math.pi / length
    )
    cosine = np.cos(phase)
    sine = np.sin(phase)
    upper_half = np.stack([cosine, -sine], axis=1)
    lower_half = np.stack([sine, cosine], axis=1)
    return np.stack([upper_half, lower_half], axis=0).astype(np.float32)


def channelise(voltages, filter_taps):
    samples = voltages[0, :, 0].astype(jnp.float32)
    taps_count = filter_taps.shape[0]
    frames = samples.shape[1] - taps_count + 1
    filtered = filter_taps[0] * samples[:, 0:frames]
    for tap_index in range(1, taps_count):
        filtered = filtered + filter_taps[tap_index] * samples[:, tap_index : tap_index + frames]
    stations = samples.shape[0]
    shaped = filtered.reshape(stations, frames, 2, ROOT, ROOT)
    matrix = fourier_segment(ROOT)
    segment_one = jnp.einsum("sfcxy,cxdk->sfdky", shaped, matrix, precision=lax.Precision.DEFAULT)
    counter = np.arange(ROOT)
    twiddle = counter[:, None] * counter[None, :] * (2.0 * math.pi / (ROOT * ROOT))
    twiddle_cos = np.cos(twiddle).astype(np.float32)
    twiddle_sin = np.sin(twiddle).astype(np.float32)
    turned_real = segment_one[:, :, 0] * twiddle_cos + segment_one[:, :, 1] * twiddle_sin
    turned_imag = segment_one[:, :, 1] * twiddle_cos - segment_one[:, :, 0] * twiddle_sin
    turned = jnp.stack([turned_real, turned_imag], axis=2)
    segment_two = jnp.einsum("sfcky,cydz->sdfzk", turned, matrix, precision=lax.Precision.DEFAULT)
    return (segment_two.reshape(stations, 2, frames, ROOT * ROOT) * (1.0 / ROOT)).astype(
        jnp.bfloat16
    )


def exchange_kernel(owners, sections, y_ref, g_ref, zs, zr, xs, xr, cs, cr, own_sem):
    z = lax.axis_index("chan")
    st = lax.axis_index("stat")
    pol = lax.axis_index("pol")

    barrier = pltpu.get_barrier_semaphore()
    for o in range(1, owners):
        pl.semaphore_signal(barrier, inc=1, device_id={"chan": lax.rem(z + o, owners)}, device_id_type=MESH)
    for o in range(1, sections):
        pl.semaphore_signal(barrier, inc=1, device_id={"stat": lax.rem(st + o, sections)}, device_id_type=MESH)
    pl.semaphore_signal(barrier, inc=1, device_id={"pol": 1 - pol}, device_id_type=MESH)
    pl.semaphore_wait(barrier, owners + sections - 1)

    def to_owner(o):
        target = lax.rem(z + o, owners)
        return pltpu.make_async_remote_copy(
            src_ref=y_ref.at[target], dst_ref=g_ref.at[0, st, z],
            send_sem=zs.at[o], recv_sem=zr.at[z],
            device_id={"chan": target}, device_id_type=MESH)

    def from_owner(o):
        source = lax.rem(z - o + owners, owners)
        return pltpu.make_async_remote_copy(
            src_ref=y_ref.at[source], dst_ref=g_ref.at[0, st, source],
            send_sem=zs.at[o], recv_sem=zr.at[source],
            device_id={"chan": source}, device_id_type=MESH)

    def to_section(o, block):
        target = lax.rem(st + o, sections)
        return pltpu.make_async_remote_copy(
            src_ref=g_ref.at[0, st, block], dst_ref=g_ref.at[0, st, block],
            send_sem=xs.at[o, block], recv_sem=xr.at[st, block],
            device_id={"stat": target}, device_id_type=MESH)

    def from_section(o, block):
        source = lax.rem(st - o + sections, sections)
        return pltpu.make_async_remote_copy(
            src_ref=g_ref.at[0, source, block], dst_ref=g_ref.at[0, source, block],
            send_sem=xs.at[o, block], recv_sem=xr.at[source, block],
            device_id={"stat": source}, device_id_type=MESH)

    def to_core(o, block):
        source = lax.rem(st - o + sections, sections)
        return pltpu.make_async_remote_copy(
            src_ref=g_ref.at[0, source, block], dst_ref=g_ref.at[1, source, block],
            send_sem=cs.at[source, block], recv_sem=cr.at[source, block],
            device_id={"pol": 1 - pol}, device_id_type=MESH)

    own = pltpu.make_async_copy(y_ref.at[z], g_ref.at[0, st, z], own_sem)
    own.start()
    for o in range(1, owners):
        to_owner(o).start()
    for o in range(owners):
        block = lax.rem(z - o + owners, owners)
        if o == 0:
            own.wait()
        else:
            from_owner(o).wait_recv()
        for q in range(1, sections):
            to_section(q, block).start()
        to_core(0, block).start()
        if o:
            before = lax.rem(z - o + 1 + owners, owners)
            for q in range(1, sections):
                from_section(q, before).wait_recv()
                to_core(q, before).start()
    last = lax.rem(z + 1, owners)
    for q in range(1, sections):
        from_section(q, last).wait_recv()
        to_core(q, last).start()
    for o in range(owners):
        for q in range(sections):
            to_core(q, lax.rem(z - o + owners, owners)).wait()
    for o in range(1, owners):
        to_owner(o).wait_send()
    for o in range(owners):
        for q in range(1, sections):
            to_section(q, lax.rem(z - o + owners, owners)).wait_send()


def exchange(blocks, owners, sections):
    return pl.pallas_call(
        functools.partial(exchange_kernel, owners, sections),
        out_shape=jax.ShapeDtypeStruct((2, sections) + blocks.shape, blocks.dtype),
        in_specs=[pl.BlockSpec(memory_space=pltpu.VMEM)],
        out_specs=pl.BlockSpec(memory_space=pltpu.VMEM),
        scratch_shapes=[
            pltpu.SemaphoreType.DMA((owners,)),
            pltpu.SemaphoreType.DMA((owners,)),
            pltpu.SemaphoreType.DMA((sections, owners)),
            pltpu.SemaphoreType.DMA((sections, owners)),
            pltpu.SemaphoreType.DMA((sections, owners)),
            pltpu.SemaphoreType.DMA((sections, owners)),
            pltpu.SemaphoreType.DMA,
        ],
        compiler_params=pltpu.CompilerParams(collective_id=0, has_side_effects=True),
        name="exchange",
    )(blocks)


def iota(shape, dim):
    return lax.broadcasted_iota(jnp.int32, shape, dim)


def product_kernel(frames, stations, mean_factor, place_ref, w_ref, col_ref, g_ref, vis_ref, out_ref, x_ref):
    _, sections, owners, groups, rows, _ = g_ref.shape
    step = pl.program_id(0)
    depth = sections * owners * rows
    pair = 4 * stations

    @pl.when(step == 0)
    def _():
        for a in range(groups):
            x_ref[:, a * AVG : (a + 1) * AVG] = g_ref[0, :, :, a].reshape(depth, AVG)

    nb = w_ref.shape[1]
    wide = jnp.dot(w_ref[0], col_ref[...], preferred_element_type=jnp.float32)
    column = iota((frames, depth), 1)
    same = lax.rem(lax.div(column, 2 * stations), frames) == iota((frames, depth), 0)
    spread = jnp.where(same[None], wide[:, None, :], 0.0).reshape(nb * frames, depth)
    out_ref[...] = jnp.dot(spread.astype(jnp.bfloat16), x_ref[...], preferred_element_type=jnp.float32)

    @pl.when(step == pl.num_programs(0) - 1)
    def _():
        st = place_ref[0]
        pol = place_ref[1]
        m = owners * pair
        n = sections * owners * pair
        own_count = owners * stations
        row = iota((m, n), 0)
        col = iota((m, n), 1)
        par = 2 * stations
        same_par = lax.rem(lax.div(row, par), 2) == lax.rem(lax.div(col, par), 2)
        rc = lax.rem(row, 2)
        cc = lax.rem(col, 2)
        re_mask = jnp.where(same_par & (rc == cc), mean_factor, 0.0)
        im_mask = jnp.where(same_par & (rc != cc), jnp.where(rc == 1, mean_factor, -mean_factor), 0.0)

        def station(i):
            return lax.div(i, pair) * stations + lax.rem(lax.div(i, 2), stations)

        left = (station(iota((own_count, m), 1)) == iota((own_count, m), 0)).astype(jnp.float32)
        inputs = sections * 2 * own_count
        for p in range(2):
            q = jnp.where(pol == 0, p, 1 - p)
            i = iota((n, inputs), 0)
            sec = lax.div(i, m)
            where = sec * (2 * own_count) + q * own_count + station(lax.rem(i, m))
            right = (where == iota((n, inputs), 1)).astype(jnp.float32)
            halves = []
            for a in range(groups):
                raw = jnp.zeros((m, n), jnp.float32)
                for f in range(rows // pair):
                    mine = g_ref[0, st, :, a, f * pair : (f + 1) * pair].reshape(m, AVG)
                    theirs = g_ref[p, :, :, a, f * pair : (f + 1) * pair].reshape(n, AVG)
                    raw = raw + lax.dot_general(
                        mine, theirs, (((1,), (1,)), ((), ())), preferred_element_type=jnp.float32
                    )
                for mask in (re_mask, im_mask):
                    halves.append(
                        jnp.dot(left, raw * mask, precision=lax.Precision.HIGHEST, preferred_element_type=jnp.float32)
                    )
            total = jnp.dot(
                jnp.concatenate(halves, axis=0), right,
                precision=lax.Precision.HIGHEST, preferred_element_type=jnp.float32,
            ).reshape(groups, 2, own_count, inputs)
            if p == 0:
                vis_ref[...] = total
            else:
                vis_ref[...] += total


def products(gathered, weights, frames, stations, mean_factor):
    _, sections, owners, groups, rows, _ = gathered.shape
    depth = sections * owners * rows
    width = groups * AVG
    count = weights.shape[0]
    nb = 50
    while count % nb or nb * frames * depth > 400 * 1024:
        nb -= 1
    blocks = count // nb
    row = jnp.arange(weights.shape[1], dtype=jnp.int32)[:, None]
    col = jnp.arange(depth, dtype=jnp.int32)[None, :]
    names = (col % 2) * (sections * owners * stations) + (col // rows) * stations + (col // 2) % stations
    spread = (row == names).astype(jnp.bfloat16)
    place = jnp.stack([lax.axis_index("stat"), lax.axis_index("pol")]).astype(jnp.int32)
    own_count = owners * stations
    vis, beams = pl.pallas_call(
        functools.partial(product_kernel, frames, stations, mean_factor),
        grid=(blocks,),
        in_specs=[
            pl.BlockSpec(memory_space=pltpu.SMEM),
            pl.BlockSpec((1, nb, weights.shape[1]), lambda i: (i, 0, 0)),
            pl.BlockSpec(memory_space=pltpu.VMEM),
            pl.BlockSpec(memory_space=pltpu.VMEM),
        ],
        out_specs=[
            pl.BlockSpec(memory_space=pltpu.VMEM),
            pl.BlockSpec((nb * frames, width), lambda i: (i, 0)),
        ],
        out_shape=[
            jax.ShapeDtypeStruct((groups, 2, own_count, 2 * sections * own_count), jnp.float32),
            jax.ShapeDtypeStruct((count * frames, width), jnp.float32),
        ],
        scratch_shapes=[pltpu.VMEM((depth, width), jnp.bfloat16)],
        compiler_params=pltpu.CompilerParams(vmem_limit_bytes=VMEM_BYTES),
        name="products",
    )(place, weights.reshape(blocks, nb, weights.shape[1]), spread, gathered)
    return vis, beams


def beam_weights(indices, beam_table, factor):
    levels = jnp.arange(beam_table.shape[1], dtype=jnp.int32)
    selected = indices[..., None] == levels
    w_real = jnp.sum(jnp.where(selected, beam_table[0], 0.0), axis=-1) * factor
    w_imag = jnp.sum(jnp.where(selected, beam_table[1], 0.0), axis=-1) * factor
    upper_half = jnp.concatenate([w_real, -w_imag], axis=1)
    lower_half = jnp.concatenate([w_imag, w_real], axis=1)
    return jnp.stack([upper_half, lower_half], axis=1).astype(jnp.bfloat16)


def on_device(voltages, filter_taps, beam_table, beam_index, block_owner):
    owners = lax.axis_size("chan")
    sections = lax.axis_size("stat")
    spectra = channelise(voltages, filter_taps)
    stations, _, frames, nfft = spectra.shape
    group_count = block_owner.shape[0]
    grouped = spectra.reshape(stations, 2, frames, group_count, AVG)
    regrouped = jnp.take(grouped, block_owner, axis=3)
    groups = group_count // owners
    blocks = jnp.transpose(regrouped, (3, 2, 0, 1, 4)).reshape(
        owners, groups, frames * stations * 2, AVG
    )
    gathered = exchange(blocks, owners, sections)
    section = lax.axis_index("stat")
    beam_count, station_count = beam_index.shape
    owned = beam_count // sections
    own_index = lax.dynamic_slice_in_dim(beam_index, section * owned, owned, 0)
    weights = beam_weights(own_index, beam_table, 1.0 / math.sqrt(station_count))
    vis, beams = products(
        gathered, weights.reshape(owned * 2, 2 * station_count), frames, stations, 1.0 / (frames * AVG)
    )
    return vis, beams.reshape(owned, 1, 2, frames, groups * AVG)


def solution(mesh):
    return jax.shard_map(
        on_device,
        mesh=mesh,
        in_specs=(P(("group", "stat"), "chan", "pol", None, None, None), P(), P(), P(), P()),
        out_specs=(
            P(("group", "chan"), None, ("stat", "pol"), None),
            P(("group", "stat"), "pol", None, None, "chan"),
        ),
        check_vma=False,
    )
```

```python
import functools
import math

import jax
import jax.numpy as jnp
import numpy as np
from jax import lax
from jax.experimental import pallas as pl
from jax.experimental.pallas import tpu as pltpu
from jax.sharding import PartitionSpec as P

ROOT = 64
AVG = 128
MESH = pl.DeviceIdType.MESH
VMEM_BYTES = 56 * 2**20


def fourier_segment(length):
    counter = np.arange(length, dtype=np.int32)
    phase = (counter[:, None] * counter[None, :] % length) * (
        2.0 * math.pi / length
    )
    cosine = np.cos(phase)
    sine = np.sin(phase)
    upper_half = np.stack([cosine, -sine], axis=1)
    lower_half = np.stack([sine, cosine], axis=1)
    return np.stack([upper_half, lower_half], axis=0).astype(np.float32)


def channelise(voltages, filter_taps):
    samples = voltages[0, :, 0].astype(jnp.float32)
    taps_count = filter_taps.shape[0]
    frames = samples.shape[1] - taps_count + 1
    filtered = filter_taps[0] * samples[:, 0:frames]
    for tap_index in range(1, taps_count):
        filtered = filtered + filter_taps[tap_index] * samples[:, tap_index : tap_index + frames]
    stations = samples.shape[0]
    shaped = filtered.reshape(stations, frames, 2, ROOT, ROOT)
    matrix = fourier_segment(ROOT)
    segment_one = jnp.einsum("sfcxy,cxdk->sfdky", shaped, matrix, precision=lax.Precision.DEFAULT)
    counter = np.arange(ROOT)
    twiddle = counter[:, None] * counter[None, :] * (2.0 * math.pi / (ROOT * ROOT))
    twiddle_cos = np.cos(twiddle).astype(np.float32)
    twiddle_sin = np.sin(twiddle).astype(np.float32)
    turned_real = segment_one[:, :, 0] * twiddle_cos + segment_one[:, :, 1] * twiddle_sin
    turned_imag = segment_one[:, :, 1] * twiddle_cos - segment_one[:, :, 0] * twiddle_sin
    turned = jnp.stack([turned_real, turned_imag], axis=2)
    segment_two = jnp.einsum("sfcky,cydz->sdfzk", turned, matrix, precision=lax.Precision.DEFAULT)
    return (segment_two.reshape(stations, 2, frames, ROOT * ROOT) * (1.0 / ROOT)).astype(
        jnp.bfloat16
    )


def exchange_kernel(owners, sections, y_ref, g_ref, zs, zr, xs, xr, cs, cr, own_sem):
    z = lax.axis_index("chan")
    st = lax.axis_index("stat")
    pol = lax.axis_index("pol")

    barrier = pltpu.get_barrier_semaphore()
    for o in range(1, owners):
        pl.semaphore_signal(barrier, inc=1, device_id={"chan": lax.rem(z + o, owners)}, device_id_type=MESH)
    for o in range(1, sections):
        pl.semaphore_signal(barrier, inc=1, device_id={"stat": lax.rem(st + o, sections)}, device_id_type=MESH)
    pl.semaphore_signal(barrier, inc=1, device_id={"pol": 1 - pol}, device_id_type=MESH)
    pl.semaphore_wait(barrier, owners + sections - 1)

    def to_owner(o):
        target = lax.rem(z + o, owners)
        return pltpu.make_async_remote_copy(
            src_ref=y_ref.at[target], dst_ref=g_ref.at[0, st, z],
            send_sem=zs.at[o], recv_sem=zr.at[z],
            device_id={"chan": target}, device_id_type=MESH)

    def from_owner(o):
        source = lax.rem(z - o + owners, owners)
        return pltpu.make_async_remote_copy(
            src_ref=y_ref.at[source], dst_ref=g_ref.at[0, st, source],
            send_sem=zs.at[o], recv_sem=zr.at[source],
            device_id={"chan": source}, device_id_type=MESH)

    def to_section(o, block):
        target = lax.rem(st + o, sections)
        return pltpu.make_async_remote_copy(
            src_ref=g_ref.at[0, st, block], dst_ref=g_ref.at[0, st, block],
            send_sem=xs.at[o, block], recv_sem=xr.at[st, block],
            device_id={"stat": target}, device_id_type=MESH)

    def from_section(o, block):
        source = lax.rem(st - o + sections, sections)
        return pltpu.make_async_remote_copy(
            src_ref=g_ref.at[0, source, block], dst_ref=g_ref.at[0, source, block],
            send_sem=xs.at[o, block], recv_sem=xr.at[source, block],
            device_id={"stat": source}, device_id_type=MESH)

    def to_core(o, block):
        source = lax.rem(st - o + sections, sections)
        return pltpu.make_async_remote_copy(
            src_ref=g_ref.at[0, source, block], dst_ref=g_ref.at[1, source, block],
            send_sem=cs.at[source, block], recv_sem=cr.at[source, block],
            device_id={"pol": 1 - pol}, device_id_type=MESH)

    own = pltpu.make_async_copy(y_ref.at[z], g_ref.at[0, st, z], own_sem)
    own.start()
    for o in range(1, owners):
        to_owner(o).start()
    for o in range(owners):
        block = lax.rem(z - o + owners, owners)
        if o == 0:
            own.wait()
        else:
            from_owner(o).wait_recv()
        for q in range(1, sections):
            to_section(q, block).start()
        to_core(0, block).start()
        if o:
            before = lax.rem(z - o + 1 + owners, owners)
            for q in range(1, sections):
                from_section(q, before).wait_recv()
                to_core(q, before).start()
    last = lax.rem(z + 1, owners)
    for q in range(1, sections):
        from_section(q, last).wait_recv()
        to_core(q, last).start()
    for o in range(owners):
        for q in range(sections):
            to_core(q, lax.rem(z - o + owners, owners)).wait()
    for o in range(1, owners):
        to_owner(o).wait_send()
    for o in range(owners):
        for q in range(1, sections):
            to_section(q, lax.rem(z - o + owners, owners)).wait_send()


def exchange(blocks, owners, sections):
    return pl.pallas_call(
        functools.partial(exchange_kernel, owners, sections),
        out_shape=jax.ShapeDtypeStruct((2, sections) + blocks.shape, blocks.dtype),
        in_specs=[pl.BlockSpec(memory_space=pl.ANY)],
        out_specs=pl.BlockSpec(memory_space=pl.ANY),
        scratch_shapes=[
            pltpu.SemaphoreType.DMA((owners,)),
            pltpu.SemaphoreType.DMA((owners,)),
            pltpu.SemaphoreType.DMA((sections, owners)),
            pltpu.SemaphoreType.DMA((sections, owners)),
            pltpu.SemaphoreType.DMA((sections, owners)),
            pltpu.SemaphoreType.DMA((sections, owners)),
            pltpu.SemaphoreType.DMA,
        ],
        compiler_params=pltpu.CompilerParams(collective_id=0, has_side_effects=True),
        name="exchange",
    )(blocks)


def iota(shape, dim):
    return lax.broadcasted_iota(jnp.int32, shape, dim)


def product_kernel(frames, stations, mean_factor, place_ref, w_ref, col_ref, g_ref, vis_ref, out_ref, x_ref):
    _, sections, owners, groups, rows, _ = g_ref.shape
    step = pl.program_id(0)
    depth = sections * owners * rows
    pair = 4 * stations

    @pl.when(step == 0)
    def _():
        for a in range(groups):
            x_ref[:, a * AVG : (a + 1) * AVG] = g_ref[0, :, :, a].reshape(depth, AVG)

    nb = w_ref.shape[1]
    wide = jnp.dot(w_ref[0], col_ref[...], preferred_element_type=jnp.float32)
    column = iota((frames, depth), 1)
    same = lax.rem(lax.div(column, 2 * stations), frames) == iota((frames, depth), 0)
    spread = jnp.where(same[None], wide[:, None, :], 0.0).reshape(nb * frames, depth)
    out_ref[...] = jnp.dot(spread.astype(jnp.bfloat16), x_ref[...], preferred_element_type=jnp.float32)

    @pl.when(step == pl.num_programs(0) - 1)
    def _():
        st = place_ref[0]
        pol = place_ref[1]
        m = owners * pair
        n = sections * owners * pair
        own_count = owners * stations
        row = iota((m, n), 0)
        col = iota((m, n), 1)
        par = 2 * stations
        same_par = lax.rem(lax.div(row, par), 2) == lax.rem(lax.div(col, par), 2)
        rc = lax.rem(row, 2)
        cc = lax.rem(col, 2)
        re_mask = jnp.where(same_par & (rc == cc), mean_factor, 0.0)
        im_mask = jnp.where(same_par & (rc != cc), jnp.where(rc == 1, mean_factor, -mean_factor), 0.0)

        def station(i):
            return lax.div(i, pair) * stations + lax.rem(lax.div(i, 2), stations)

        left = (station(iota((own_count, m), 1)) == iota((own_count, m), 0)).astype(jnp.float32)
        inputs = sections * 2 * own_count
        for p in range(2):
            q = jnp.where(pol == 0, p, 1 - p)
            i = iota((n, inputs), 0)
            sec = lax.div(i, m)
            where = sec * (2 * own_count) + q * own_count + station(lax.rem(i, m))
            right = (where == iota((n, inputs), 1)).astype(jnp.float32)
            halves = []
            for a in range(groups):
                raw = jnp.zeros((m, n), jnp.float32)
                for f in range(rows // pair):
                    mine = g_ref[0, st, :, a, f * pair : (f + 1) * pair].reshape(m, AVG)
                    theirs = g_ref[p, :, :, a, f * pair : (f + 1) * pair].reshape(n, AVG)
                    raw = raw + lax.dot_general(
                        mine, theirs, (((1,), (1,)), ((), ())), preferred_element_type=jnp.float32
                    )
                for mask in (re_mask, im_mask):
                    halves.append(
                        jnp.dot(left, raw * mask, precision=lax.Precision.HIGHEST, preferred_element_type=jnp.float32)
                    )
            total = jnp.dot(
                jnp.concatenate(halves, axis=0), right,
                precision=lax.Precision.HIGHEST, preferred_element_type=jnp.float32,
            ).reshape(groups, 2, own_count, inputs)
            if p == 0:
                vis_ref[...] = total
            else:
                vis_ref[...] += total


def products(gathered, weights, frames, stations, mean_factor):
    _, sections, owners, groups, rows, _ = gathered.shape
    depth = sections * owners * rows
    width = groups * AVG
    count = weights.shape[0]
    nb = 50
    while count % nb or nb * frames * depth > 400 * 1024:
        nb -= 1
    blocks = count // nb
    row = jnp.arange(weights.shape[1], dtype=jnp.int32)[:, None]
    col = jnp.arange(depth, dtype=jnp.int32)[None, :]
    names = (col % 2) * (sections * owners * stations) + (col // rows) * stations + (col // 2) % stations
    spread = (row == names).astype(jnp.bfloat16)
    place = jnp.stack([lax.axis_index("stat"), lax.axis_index("pol")]).astype(jnp.int32)
    own_count = owners * stations
    vis, beams = pl.pallas_call(
        functools.partial(product_kernel, frames, stations, mean_factor),
        grid=(blocks,),
        in_specs=[
            pl.BlockSpec(memory_space=pltpu.SMEM),
            pl.BlockSpec((1, nb, weights.shape[1]), lambda i: (i, 0, 0)),
            pl.BlockSpec(memory_space=pltpu.VMEM),
            pl.BlockSpec(memory_space=pltpu.VMEM),
        ],
        out_specs=[
            pl.BlockSpec(memory_space=pltpu.VMEM),
            pl.BlockSpec((nb * frames, width), lambda i: (i, 0)),
        ],
        out_shape=[
            jax.ShapeDtypeStruct((groups, 2, own_count, 2 * sections * own_count), jnp.float32),
            jax.ShapeDtypeStruct((count * frames, width), jnp.float32),
        ],
        scratch_shapes=[pltpu.VMEM((depth, width), jnp.bfloat16)],
        compiler_params=pltpu.CompilerParams(vmem_limit_bytes=VMEM_BYTES),
        name="products",
    )(place, weights.reshape(blocks, nb, weights.shape[1]), spread, gathered)
    return vis, beams


def beam_weights(indices, beam_table, factor):
    w_real = jnp.zeros(indices.shape, jnp.float32)
    w_imag = w_real
    for level in range(beam_table.shape[1]):
        selected = indices == level
        w_real = jnp.where(selected, beam_table[0, level], w_real)
        w_imag = jnp.where(selected, beam_table[1, level], w_imag)
    w_real = w_real * factor
    w_imag = w_imag * factor
    upper_half = jnp.concatenate([w_real, -w_imag], axis=1)
    lower_half = jnp.concatenate([w_imag, w_real], axis=1)
    return jnp.stack([upper_half, lower_half], axis=1).astype(jnp.bfloat16)


def on_device(voltages, filter_taps, beam_table, beam_index, block_owner):
    owners = lax.axis_size("chan")
    sections = lax.axis_size("stat")
    spectra = channelise(voltages, filter_taps)
    stations, _, frames, nfft = spectra.shape
    group_count = block_owner.shape[0]
    grouped = spectra.reshape(stations, 2, frames, group_count, AVG)
    regrouped = jnp.take(grouped, block_owner, axis=3)
    groups = group_count // owners
    blocks = jnp.transpose(regrouped, (3, 2, 0, 1, 4)).reshape(
        owners, groups, frames * stations * 2, AVG
    )
    gathered = exchange(blocks, owners, sections)
    section = lax.axis_index("stat")
    beam_count, station_count = beam_index.shape
    owned = beam_count // sections
    own_index = lax.dynamic_slice_in_dim(beam_index, section * owned, owned, 0)
    weights = beam_weights(own_index, beam_table, 1.0 / math.sqrt(station_count))
    vis, beams = products(
        gathered, weights.reshape(owned * 2, 2 * station_count), frames, stations, 1.0 / (frames * AVG)
    )
    return vis, beams.reshape(owned, 1, 2, frames, groups * AVG)


def solution(mesh):
    return jax.shard_map(
        on_device,
        mesh=mesh,
        in_specs=(P(("group", "stat"), "chan", "pol", None, None, None), P(), P(), P(), P()),
        out_specs=(
            P(("group", "chan"), None, ("stat", "pol"), None),
            P(("group", "stat"), "pol", None, None, "chan"),
        ),
        check_vma=False,
    )
```

```python
import functools
import math

import jax
import jax.numpy as jnp
import numpy as np
from jax import lax
from jax.experimental import pallas as pl
from jax.experimental.pallas import tpu as pltpu
from jax.sharding import PartitionSpec as P

ROOT = 64
AVG = 128
MESH = pl.DeviceIdType.MESH
VMEM_BYTES = 56 * 2**20


def fourier_segment(length):
    counter = np.arange(length, dtype=np.int32)
    phase = (counter[:, None] * counter[None, :] % length) * (
        2.0 * math.pi / length
    )
    cosine = np.cos(phase)
    sine = np.sin(phase)
    upper_half = np.stack([cosine, -sine], axis=1)
    lower_half = np.stack([sine, cosine], axis=1)
    return np.stack([upper_half, lower_half], axis=0).astype(np.float32)


def channelise(voltages, filter_taps):
    samples = voltages[0, :, 0].astype(jnp.float32)
    taps_count = filter_taps.shape[0]
    frames = samples.shape[1] - taps_count + 1
    filtered = filter_taps[0] * samples[:, 0:frames]
    for tap_index in range(1, taps_count):
        filtered = filtered + filter_taps[tap_index] * samples[:, tap_index : tap_index + frames]
    stations = samples.shape[0]
    shaped = filtered.reshape(stations, frames, 2, ROOT, ROOT)
    matrix = fourier_segment(ROOT)
    segment_one = jnp.einsum("sfcxy,cxdk->sfdky", shaped, matrix, precision=lax.Precision.DEFAULT)
    counter = np.arange(ROOT)
    twiddle = counter[:, None] * counter[None, :] * (2.0 * math.pi / (ROOT * ROOT))
    twiddle_cos = np.cos(twiddle).astype(np.float32)
    twiddle_sin = np.sin(twiddle).astype(np.float32)
    turned_real = segment_one[:, :, 0] * twiddle_cos + segment_one[:, :, 1] * twiddle_sin
    turned_imag = segment_one[:, :, 1] * twiddle_cos - segment_one[:, :, 0] * twiddle_sin
    turned = jnp.stack([turned_real, turned_imag], axis=2)
    segment_two = jnp.einsum("sfcky,cydz->sdfzk", turned, matrix, precision=lax.Precision.DEFAULT)
    return (segment_two.reshape(stations, 2, frames, ROOT * ROOT) * (1.0 / ROOT)).astype(
        jnp.bfloat16
    )


def exchange_kernel(owners, sections, y_ref, g_ref, zs, zr, xs, xr, cs, cr, own_sem):
    z = lax.axis_index("chan")
    st = lax.axis_index("stat")
    pol = lax.axis_index("pol")

    barrier = pltpu.get_barrier_semaphore()
    for o in range(1, owners):
        pl.semaphore_signal(barrier, inc=1, device_id={"chan": lax.rem(z + o, owners)}, device_id_type=MESH)
    for o in range(1, sections):
        pl.semaphore_signal(barrier, inc=1, device_id={"stat": lax.rem(st + o, sections)}, device_id_type=MESH)
    pl.semaphore_signal(barrier, inc=1, device_id={"pol": 1 - pol}, device_id_type=MESH)
    pl.semaphore_wait(barrier, owners + sections - 1)

    def to_owner(o):
        target = lax.rem(z + o, owners)
        return pltpu.make_async_remote_copy(
            src_ref=y_ref.at[target], dst_ref=g_ref.at[0, st, z],
            send_sem=zs.at[o], recv_sem=zr.at[z],
            device_id={"chan": target}, device_id_type=MESH)

    def from_owner(o):
        source = lax.rem(z - o + owners, owners)
        return pltpu.make_async_remote_copy(
            src_ref=y_ref.at[source], dst_ref=g_ref.at[0, st, source],
            send_sem=zs.at[o], recv_sem=zr.at[source],
            device_id={"chan": source}, device_id_type=MESH)

    def to_section(o, block):
        target = lax.rem(st + o, sections)
        return pltpu.make_async_remote_copy(
            src_ref=g_ref.at[0, st, block], dst_ref=g_ref.at[0, st, block],
            send_sem=xs.at[o, block], recv_sem=xr.at[st, block],
            device_id={"stat": target}, device_id_type=MESH)

    def from_section(o, block):
        source = lax.rem(st - o + sections, sections)
        return pltpu.make_async_remote_copy(
            src_ref=g_ref.at[0, source, block], dst_ref=g_ref.at[0, source, block],
            send_sem=xs.at[o, block], recv_sem=xr.at[source, block],
            device_id={"stat": source}, device_id_type=MESH)

    def to_core(o, block):
        source = lax.rem(st - o + sections, sections)
        return pltpu.make_async_remote_copy(
            src_ref=g_ref.at[0, source, block], dst_ref=g_ref.at[1, source, block],
            send_sem=cs.at[source, block], recv_sem=cr.at[source, block],
            device_id={"pol": 1 - pol}, device_id_type=MESH)

    own = pltpu.make_async_copy(y_ref.at[z], g_ref.at[0, st, z], own_sem)
    own.start()
    for o in range(1, owners):
        to_owner(o).start()
    for o in range(owners):
        block = lax.rem(z - o + owners, owners)
        if o == 0:
            own.wait()
        else:
            from_owner(o).wait_recv()
        for q in range(1, sections):
            to_section(q, block).start()
        to_core(0, block).start()
        if o:
            before = lax.rem(z - o + 1 + owners, owners)
            for q in range(1, sections):
                from_section(q, before).wait_recv()
                to_core(q, before).start()
    last = lax.rem(z + 1, owners)
    for q in range(1, sections):
        from_section(q, last).wait_recv()
        to_core(q, last).start()
    for o in range(owners):
        for q in range(sections):
            to_core(q, lax.rem(z - o + owners, owners)).wait()
    for o in range(1, owners):
        to_owner(o).wait_send()
    for o in range(owners):
        for q in range(1, sections):
            to_section(q, lax.rem(z - o + owners, owners)).wait_send()


def exchange(blocks, owners, sections):
    return pl.pallas_call(
        functools.partial(exchange_kernel, owners, sections),
        out_shape=jax.ShapeDtypeStruct((2, sections) + blocks.shape, blocks.dtype),
        in_specs=[pl.BlockSpec(memory_space=pl.ANY)],
        out_specs=pl.BlockSpec(memory_space=pl.ANY),
        scratch_shapes=[
            pltpu.SemaphoreType.DMA((owners,)),
            pltpu.SemaphoreType.DMA((owners,)),
            pltpu.SemaphoreType.DMA((sections, owners)),
            pltpu.SemaphoreType.DMA((sections, owners)),
            pltpu.SemaphoreType.DMA((sections, owners)),
            pltpu.SemaphoreType.DMA((sections, owners)),
            pltpu.SemaphoreType.DMA,
        ],
        compiler_params=pltpu.CompilerParams(collective_id=0, has_side_effects=True),
        name="exchange",
    )(blocks)


def iota(shape, dim):
    return lax.broadcasted_iota(jnp.int32, shape, dim)


def product_kernel(frames, stations, mean_factor, place_ref, w_ref, col_ref, g_ref, vis_ref, out_ref, x_ref):
    _, sections, owners, groups, rows, _ = g_ref.shape
    step = pl.program_id(0)
    depth = sections * owners * rows
    pair = 4 * stations

    @pl.when(step == 0)
    def _():
        for a in range(groups):
            x_ref[:, a * AVG : (a + 1) * AVG] = g_ref[0, :, :, a].reshape(depth, AVG)

    nb = w_ref.shape[1]
    wide = jnp.dot(w_ref[0], col_ref[...], preferred_element_type=jnp.float32)
    column = iota((frames, depth), 1)
    same = lax.rem(lax.div(column, 2 * stations), frames) == iota((frames, depth), 0)
    spread = jnp.where(same[None], wide[:, None, :], 0.0).reshape(nb * frames, depth)
    out_ref[...] = jnp.dot(spread.astype(jnp.bfloat16), x_ref[...], preferred_element_type=jnp.float32)

    @pl.when(step == pl.num_programs(0) - 1)
    def _():
        st = place_ref[0]
        pol = place_ref[1]
        m = owners * pair
        n = sections * owners * pair
        own_count = owners * stations
        row = iota((m, n), 0)
        col = iota((m, n), 1)
        par = 2 * stations
        same_par = lax.rem(lax.div(row, par), 2) == lax.rem(lax.div(col, par), 2)
        rc = lax.rem(row, 2)
        cc = lax.rem(col, 2)
        re_mask = jnp.where(same_par & (rc == cc), mean_factor, 0.0)
        im_mask = jnp.where(same_par & (rc != cc), jnp.where(rc == 1, mean_factor, -mean_factor), 0.0)

        def station(i):
            return lax.div(i, pair) * stations + lax.rem(lax.div(i, 2), stations)

        left = (station(iota((own_count, m), 1)) == iota((own_count, m), 0)).astype(jnp.float32)
        inputs = sections * 2 * own_count
        for p in range(2):
            q = jnp.where(pol == 0, p, 1 - p)
            i = iota((n, inputs), 0)
            sec = lax.div(i, m)
            where = sec * (2 * own_count) + q * own_count + station(lax.rem(i, m))
            right = (where == iota((n, inputs), 1)).astype(jnp.float32)
            halves = []
            for a in range(groups):
                raw = jnp.zeros((m, n), jnp.float32)
                for f in range(rows // pair):
                    mine = g_ref[0, st, :, a, f * pair : (f + 1) * pair].reshape(m, AVG)
                    theirs = g_ref[p, :, :, a, f * pair : (f + 1) * pair].reshape(n, AVG)
                    raw = raw + lax.dot_general(
                        mine, theirs, (((1,), (1,)), ((), ())), preferred_element_type=jnp.float32
                    )
                for mask in (re_mask, im_mask):
                    halves.append(
                        jnp.dot(left, raw * mask, precision=lax.Precision.HIGHEST, preferred_element_type=jnp.float32)
                    )
            total = jnp.dot(
                jnp.concatenate(halves, axis=0), right,
                precision=lax.Precision.HIGHEST, preferred_element_type=jnp.float32,
            ).reshape(groups, 2, own_count, inputs)
            if p == 0:
                vis_ref[...] = total
            else:
                vis_ref[...] += total


def products(gathered, weights, frames, stations, mean_factor):
    _, sections, owners, groups, rows, _ = gathered.shape
    depth = sections * owners * rows
    width = groups * AVG
    count = weights.shape[0]
    nb = 100
    while count % nb or nb * frames * depth > 400 * 1024:
        nb -= 1
    blocks = count // nb
    row = jnp.arange(weights.shape[1], dtype=jnp.int32)[:, None]
    col = jnp.arange(depth, dtype=jnp.int32)[None, :]
    names = (col % 2) * (sections * owners * stations) + (col // rows) * stations + (col // 2) % stations
    spread = (row == names).astype(jnp.bfloat16)
    place = jnp.stack([lax.axis_index("stat"), lax.axis_index("pol")]).astype(jnp.int32)
    own_count = owners * stations
    vis, beams = pl.pallas_call(
        functools.partial(product_kernel, frames, stations, mean_factor),
        grid=(blocks,),
        in_specs=[
            pl.BlockSpec(memory_space=pltpu.SMEM),
            pl.BlockSpec((1, nb, weights.shape[1]), lambda i: (i, 0, 0)),
            pl.BlockSpec(memory_space=pltpu.VMEM),
            pl.BlockSpec(memory_space=pltpu.VMEM),
        ],
        out_specs=[
            pl.BlockSpec(memory_space=pltpu.VMEM),
            pl.BlockSpec((nb * frames, width), lambda i: (i, 0)),
        ],
        out_shape=[
            jax.ShapeDtypeStruct((groups, 2, own_count, 2 * sections * own_count), jnp.float32),
            jax.ShapeDtypeStruct((count * frames, width), jnp.float32),
        ],
        scratch_shapes=[pltpu.VMEM((depth, width), jnp.bfloat16)],
        compiler_params=pltpu.CompilerParams(vmem_limit_bytes=VMEM_BYTES),
        name="products",
    )(place, weights.reshape(blocks, nb, weights.shape[1]), spread, gathered)
    return vis, beams


def beam_weights(indices, beam_table, factor):
    levels = jnp.arange(beam_table.shape[1], dtype=jnp.int32)
    selected = indices[..., None] == levels
    w_real = jnp.sum(jnp.where(selected, beam_table[0], 0.0), axis=-1) * factor
    w_imag = jnp.sum(jnp.where(selected, beam_table[1], 0.0), axis=-1) * factor
    upper_half = jnp.concatenate([w_real, -w_imag], axis=1)
    lower_half = jnp.concatenate([w_imag, w_real], axis=1)
    return jnp.stack([upper_half, lower_half], axis=1).astype(jnp.bfloat16)


def on_device(voltages, filter_taps, beam_table, beam_index, block_owner):
    owners = lax.axis_size("chan")
    sections = lax.axis_size("stat")
    spectra = channelise(voltages, filter_taps)
    stations, _, frames, nfft = spectra.shape
    group_count = block_owner.shape[0]
    grouped = spectra.reshape(stations, 2, frames, group_count, AVG)
    regrouped = jnp.take(grouped, block_owner, axis=3)
    groups = group_count // owners
    blocks = jnp.transpose(regrouped, (3, 2, 0, 1, 4)).reshape(
        owners, groups, frames * stations * 2, AVG
    )
    gathered = exchange(blocks, owners, sections)
    section = lax.axis_index("stat")
    beam_count, station_count = beam_index.shape
    owned = beam_count // sections
    own_index = lax.dynamic_slice_in_dim(beam_index, section * owned, owned, 0)
    weights = beam_weights(own_index, beam_table, 1.0 / math.sqrt(station_count))
    vis, beams = products(
        gathered, weights.reshape(owned * 2, 2 * station_count), frames, stations, 1.0 / (frames * AVG)
    )
    return vis, beams.reshape(owned, 1, 2, frames, groups * AVG)


def solution(mesh):
    return jax.shard_map(
        on_device,
        mesh=mesh,
        in_specs=(P(("group", "stat"), "chan", "pol", None, None, None), P(), P(), P(), P()),
        out_specs=(
            P(("group", "chan"), None, ("stat", "pol"), None),
            P(("group", "stat"), "pol", None, None, "chan"),
        ),
        check_vma=False,
    )
```
